32 devices in a mesh: chan: 4 (over y, x), kin: 8 (over z, core).
Axes of the slice: x: 2, y: 2, z: 4, core: 2. Of those that a mesh axis runs over, the one named last changes fastest.
Arguments:
- amplitudes: bfloat16 [256, 512, 512], P(('chan', 'kin')), may hold values from -0.25 to 0.25
- coulomb: bfloat16 [256, 512, 512], P(('chan', 'kin')), may hold values from -6 to 6
- energies: float32 [256, 512], P(('chan', 'kin')), may hold values from 0.5 to 3
- orders: int32 [256], P(('chan', 'kin')), may hold values from 384 to 512, as said below
- partner: int32 [256], P(('chan', 'kin')), may hold values from 0 to 255, as said below
- listed: int32 [512], P(('chan', 'kin')), may hold values from 0 to 122, as said below
- mate_piece: int32 [512], P(('chan', 'kin')), may hold values from 0 to 127, as said below
Outputs:
- updated: bfloat16 [256, 512, 512], P(('chan', 'kin'))
The draws below stay inside these ranges and needn't reach their ends.
Inputs may be any that keep to these rules, and one draw needn't show every extreme that they name: `orders`: each channel's order is one of 384, 448 and 512; a channel and its partner have the same order. partner is an involution without fixed points; the partner of a channel held by the device with chan index i and kin index k is held by the device with chan index i xor (2) and the same kin index. `listed`: the 16 entries of one device are distinct tiles whose tile row and tile column are both below 3. `mate_piece`: the mate relation is an involution without fixed points among the listed pieces of the devices of one chan index; at most 4 pieces of one device have their mates on any one device (itself included), and in every chan index some pair of devices reaches 4.
All inputs are finite; a program needn't handle non-finite values.
Results may differ from the reference program's by a relative error of at most 0.006.
Values may be sent and summed in bfloat16 or wider, within the bound.
A program may use at most 128 MiB of HBM per device.

```python
import math
import jax
import jax.numpy as jnp
from jax import lax

NMAX = 512
TILE = 128
CH_DEV = 8
PIECES = 16
CHANNELS = 256
N_CHAN = 4
N_KIN = 8


def channel_tables(key):
    half_chan = N_CHAN // 2
    groups = half_chan * N_KIN
    subkeys = jax.random.split(jax.random.fold_in(key, 11), groups)
    pairing = jax.vmap(lambda subkey: jax.random.permutation(subkey, CH_DEV))(subkeys).astype(jnp.int32)
    inverse = jnp.argsort(pairing, axis=1).astype(jnp.int32)
    levels = jax.random.randint(jax.random.fold_in(key, 12), (groups, CH_DEV), 0, 3).astype(jnp.int32)
    levels = levels.at[0, 0].set(0)
    levels = levels.at[0, 1].set(2)
    channel = jnp.arange(CHANNELS, dtype=jnp.int32)
    device = channel // CH_DEV
    slot_index = channel % CH_DEV
    chan_row = device // N_KIN
    kin_index = device % N_KIN
    upper = chan_row >= half_chan
    group_index = chan_row % half_chan * N_KIN + kin_index
    mate_row = jnp.where(upper, chan_row - half_chan, chan_row + half_chan)
    mate_slot = jnp.where(upper, inverse[group_index, slot_index], pairing[group_index, slot_index])
    partner_channel = (mate_row * N_KIN + kin_index) * CH_DEV + mate_slot
    lower_slot = jnp.where(upper, inverse[group_index, slot_index], slot_index)
    order_value = NMAX - levels[group_index, lower_slot] * (NMAX // 8)
    return (order_value.astype(jnp.int32), partner_channel.astype(jnp.int32))


def draw_orders(key, part):
    return channel_tables(key)[0]


def draw_partner(key, part):
    return channel_tables(key)[1]


def piece_tables(key):
    devices = N_CHAN * N_KIN
    valid_count = CH_DEV * 9
    subkeys = jax.random.split(jax.random.fold_in(key, 21), devices)
    choose = jax.vmap(lambda subkey: jax.random.permutation(subkey, valid_count)[:PIECES])(subkeys).astype(jnp.int32)
    listed_tiles = choose // 9 * 16 + choose % 9 // 3 * 4 + choose % 3
    order_keys = jax.random.split(jax.random.fold_in(key, 22), devices)
    placing = jax.vmap(lambda subkey: jax.random.permutation(subkey, PIECES))(order_keys).astype(jnp.int32)
    split_draw = jax.random.randint(jax.random.fold_in(key, 23), (N_CHAN, N_KIN // 2), 0, 3).astype(jnp.int32) * 2
    leading = jax.random.randint(jax.random.fold_in(key, 24), (N_CHAN,), 0, 2).astype(jnp.int32) * 4
    split_draw = split_draw.at[:, 0].set(leading)
    lane_sizes = jnp.stack([split_draw, 4 - split_draw], axis=2).reshape(N_CHAN, N_KIN)
    lane_end = jnp.cumsum(lane_sizes, axis=1).astype(jnp.int32)
    lane_first = lane_end - lane_sizes
    device = jnp.arange(devices, dtype=jnp.int32)
    chan_row = device // N_KIN
    kin_index = device % N_KIN
    position = jnp.arange(PIECES, dtype=jnp.int32)
    lane_index = jnp.sum((lane_end[chan_row][:, None, :] <= position[None, :, None]).astype(jnp.int32), axis=2).astype(jnp.int32)
    lane_start = jnp.take_along_axis(lane_first[chan_row], lane_index, axis=1)
    offset = position[None, :] - lane_start
    peer_kin = (lane_index - kin_index[:, None]) % N_KIN
    mate_offset = jnp.where(peer_kin == kin_index[:, None], offset + 1 - 2 * (offset % 2), offset)
    mate_position = lane_start + mate_offset
    mate_device = chan_row[:, None] * N_KIN + peer_kin
    mate_index = placing[mate_device, mate_position]
    mate_value = (peer_kin * PIECES + mate_index).astype(jnp.int32)
    mate_table = jnp.zeros((devices, PIECES), jnp.int32)
    mate_table = mate_table.at[device[:, None], placing].set(mate_value)
    return (listed_tiles.reshape(-1).astype(jnp.int32), mate_table.reshape(-1).astype(jnp.int32))


def draw_listed(key, part):
    return piece_tables(key)[0]


def draw_mate_piece(key, part):
    return piece_tables(key)[1]


def block_levels(own_key, shape, shards, smallest, high):
    def one(axis_at, blocks):
        draws = jax.random.uniform(jax.random.fold_in(jax.random.fold_in(own_key, 6), axis_at), (blocks,), jnp.float32, smallest / len(shards), high / len(shards))
        return jnp.repeat(jnp.exp(draws), shape[axis_at] // blocks).reshape((-1,) + (1,) * (len(shape) - axis_at - 1))

    level = one(*shards[0])
    for cut in shards[1:]:
        level = level * one(*cut)
    return level


def centred(key, shape, spread, most, cuts=(), kind=jnp.bfloat16):
    array = spread * jax.random.normal(key, shape, jnp.float32)
    if cuts:
        array = array * block_levels(key, shape, cuts, -0.22, 0.18)
    return jnp.clip(array, -most, most).astype(kind)


def setup_inputs(seed: int = 0) -> dict:
    seeds = jax.random.split(jax.random.key(seed), 8)
    amplitudes = centred(seeds[0], (CHANNELS, NMAX, NMAX), NMAX ** -0.5, 0.25, ((0, 32),))
    coulomb = centred(seeds[1], (CHANNELS, NMAX, NMAX), 1.0, 6.0, ((0, 32),))
    energies = jnp.clip(jnp.exp(math.log(3.0) - 1.7917595 * jax.random.uniform(seeds[2], (CHANNELS, NMAX), jnp.float32) ** block_levels(seeds[2], (CHANNELS, NMAX), ((0, 32),), -0.2, 0.2)), 0.5, 3.0)
    orders = draw_orders(jax.random.fold_in(seeds[7], 71), 0)
    partner = draw_partner(jax.random.fold_in(seeds[7], 71), 0)
    listed = draw_listed(jax.random.fold_in(seeds[7], 71), 0)
    mate_piece = draw_mate_piece(jax.random.fold_in(seeds[7], 71), 0)
    return dict(amplitudes=amplitudes, coulomb=coulomb, energies=energies, orders=orders, partner=partner, listed=listed, mate_piece=mate_piece)


def block_mask(order_value):
    indices = jnp.arange(NMAX, dtype=jnp.int32)
    inside = indices < order_value
    return inside[:, None] & inside[None, :]


def cycle_residual(operands):
    amp_block, coul_block, order_value = operands
    keep_mask = block_mask(order_value)
    amp_kept = jnp.where(keep_mask, amp_block, jnp.zeros_like(amp_block))
    coul_kept = jnp.where(keep_mask, coul_block, jnp.zeros_like(coul_block))
    forward = jnp.dot(amp_kept, coul_kept, preferred_element_type=jnp.float32)
    forward_half = forward.astype(jnp.bfloat16)
    backward = jnp.dot(coul_kept, amp_kept, preferred_element_type=jnp.float32)
    sandwich = jnp.dot(forward_half, amp_kept, preferred_element_type=jnp.float32)
    return (coul_kept.astype(jnp.float32) + backward + forward + sandwich).astype(jnp.bfloat16)


def reference(amplitudes, coulomb, energies, orders, partner, listed, mate_piece):
    residual = lax.map(cycle_residual, (amplitudes, coulomb, orders))

    def symmetrize(operands):
        own_block, partner_index = operands
        mirror = lax.dynamic_index_in_dim(residual, partner_index.astype(jnp.int32), 0, keepdims=False)
        total = 0.5 * (own_block.astype(jnp.float32) + mirror.T.astype(jnp.float32))
        return total.astype(jnp.bfloat16)

    coupled = lax.map(symmetrize, (residual, partner))
    channels = coupled.shape[0]
    tile_stack = coupled.reshape(channels, 4, TILE, 4, TILE).transpose(0, 1, 3, 2, 4).reshape(channels * 16, TILE, TILE)
    piece_ids = jnp.arange(listed.shape[0], dtype=jnp.int32)
    owner_device = piece_ids // PIECES
    tile_ids = ((owner_device * CH_DEV + listed // 16) * 16 + listed % 16).astype(jnp.int32)
    mate_ids = ((owner_device // N_KIN) * (N_KIN * PIECES) + mate_piece).astype(jnp.int32)
    piece_tiles = tile_stack[tile_ids]
    mate_tiles = piece_tiles[mate_ids]
    exchanged = tile_stack.astype(jnp.float32).at[tile_ids].add(-jnp.swapaxes(mate_tiles, 1, 2).astype(jnp.float32))
    unfolded = exchanged.reshape(channels, 4, 4, TILE, TILE).transpose(0, 1, 3, 2, 4).reshape(channels, NMAX, NMAX)

    def finish(operands):
        unfolded_block, energy_row, order_value = operands
        denominator = energy_row[:, None] + energy_row[None, :]
        return jnp.where(block_mask(order_value), unfolded_block / denominator, jnp.zeros_like(unfolded_block)).astype(jnp.bfloat16)

    return lax.map(finish, (unfolded, energies, orders))
```

```python
import functools

import jax
import jax.numpy as jnp
from jax import lax
from jax.experimental import pallas as pl
from jax.experimental.pallas import tpu as pltpu
from jax.sharding import PartitionSpec as P

MESH = pl.DeviceIdType.MESH
CAP = 4
SIDE = 4
LISTED = 3
F32 = jnp.float32
BF16 = jnp.bfloat16


def exchange_kernel(
    n_chan, n_kin, orders, partner, listed, mate, amp_hbm, coul_hbm,
    coupled_out, low_out, right_out, mlow_out, mright_out, incoming_out, slots_out,
    amp, coul, own_in, own_low, own_right, sent_in, sent_low, sent_right,
    mirror_in, coupled, outgoing,
    load_sem, keep_sem, send_sem, recv_sem, kin_send, kin_recv, own_sem,
):
    channels, order, _ = amp.shape
    tile = order // SIDE
    inner = LISTED * tile
    pieces = listed.shape[0]
    chan = lax.axis_index("chan")
    kin = lax.axis_index("kin")
    across = lax.rem(chan + n_chan // 2, n_chan)

    def load(c):
        return (
            pltpu.make_async_copy(amp_hbm.at[c], amp.at[c], load_sem.at[0, c]),
            pltpu.make_async_copy(coul_hbm.at[c], coul.at[c], load_sem.at[1, c]),
        )

    def remote(src, dst, part, c):
        return pltpu.make_async_remote_copy(
            src_ref=src.at[c], dst_ref=dst.at[c], send_sem=send_sem.at[part, c],
            recv_sem=recv_sem.at[part, c], device_id=(across, kin), device_id_type=MESH,
        )

    def send_inner(c):
        return remote(sent_in, mirror_in, 0, c)

    def send_rest(c):
        return (remote(sent_low, mlow_out, 1, c), remote(sent_right, mright_out, 2, c))

    @pl.loop(0, channels)
    def _(c):
        for copy in load(c):
            copy.start()

    barrier = pltpu.get_barrier_semaphore()
    pl.semaphore_signal(barrier, inc=1, device_id=(across, kin), device_id_type=MESH)

    @pl.loop(1, n_kin)
    def _(d):
        pl.semaphore_signal(
            barrier, inc=1, device_id=(chan, lax.rem(kin + d, n_kin)), device_id_type=MESH
        )

    pl.semaphore_wait(barrier, n_kin)

    @pl.loop(0, channels)
    def _(c):
        for copy in load(c):
            copy.wait()
        count = orders[c]
        keep = (lax.broadcasted_iota(jnp.int32, (order, order), 0) < count) & (
            lax.broadcasted_iota(jnp.int32, (order, order), 1) < count
        )
        t = jnp.where(keep, amp[c].astype(F32), 0.0).astype(BF16)
        v = jnp.where(keep, coul[c].astype(F32), 0.0).astype(BF16)
        amp[c] = t
        coul[c] = v
        for half in range(2):
            rows = pl.ds(half * (order // 2), order // 2)
            ahead = coul[c, rows, :].astype(F32) + jnp.dot(
                amp[c, rows, :], coul[c], preferred_element_type=F32
            )
            total = ahead + jnp.dot(ahead.astype(BF16), amp[c], preferred_element_type=F32)
            residual = total.astype(BF16)
            flipped = residual.T
            for i in range(SIDE // 2):
                at = half * (SIDE // 2) + i
                span = slice(at * tile, (at + 1) * tile)
                row = residual[i * tile : (i + 1) * tile, :]
                col = flipped[:, i * tile : (i + 1) * tile]
                sent_low[c, :, span] = col[inner:, :]
                if at < LISTED:
                    for j in range(LISTED):
                        part = slice(j * tile, (j + 1) * tile)
                        own_in[c, at, j] = row[:, part]
                        sent_in[c, j, at] = col[part, :]
                    own_right[c, span, :] = row[:, inner:]
                else:
                    own_low[c] = row
                    sent_right[c] = col[:inner, :]
        send_inner(c).start()

    keeps = (
        pltpu.make_async_copy(own_low, low_out, keep_sem.at[0]),
        pltpu.make_async_copy(own_right, right_out, keep_sem.at[1]),
    )
    for copy in keeps:
        copy.start()

    @pl.loop(0, channels - 1)
    def _(c):
        send_inner(c).wait_recv()

    for copy in send_rest(0):
        copy.start()
    send_inner(channels - 1).wait_recv()

    @pl.loop(1, channels)
    def _(c):
        for copy in send_rest(c):
            copy.start()

    @pl.loop(0, channels)
    def _(c):
        mirror = lax.rem(partner[c], channels)
        for i in range(LISTED):
            for j in range(LISTED):
                total = own_in[c, i, j].astype(F32) + mirror_in[mirror, i, j].astype(F32)
                coupled[c, i, j] = (0.5 * total).astype(BF16)

    keep_coupled = pltpu.make_async_copy(coupled, coupled_out, keep_sem.at[2])
    keep_coupled.start()

    @pl.loop(0, n_kin)
    def _(peer):
        def pick(p, state):
            met, *chosen = state
            hit = lax.div(mate[p], pieces) == peer
            chosen = [jnp.where(hit & (met == j), listed[p], s) for j, s in enumerate(chosen)]
            return (met + hit.astype(jnp.int32), *chosen)

        zero = jnp.int32(0)
        _, *chosen = lax.fori_loop(0, pieces, pick, (zero,) * (CAP + 1))
        for j, at in enumerate(chosen):
            spot = lax.rem(at, SIDE * SIDE)
            outgoing[peer, j] = coupled[
                lax.div(at, SIDE * SIDE), lax.div(spot, SIDE), lax.rem(spot, SIDE)
            ].T

    def to_peer(d, src, dst):
        return pltpu.make_async_remote_copy(
            src_ref=outgoing.at[src], dst_ref=incoming_out.at[dst], send_sem=kin_send.at[d],
            recv_sem=kin_recv.at[d], device_id=(chan, src), device_id_type=MESH,
        )

    @pl.loop(1, n_kin)
    def _(d):
        to_peer(d, lax.rem(kin + d, n_kin), kin).start()

    stays = pltpu.make_async_copy(outgoing.at[kin], incoming_out.at[kin], own_sem)
    stays.start()

    @pl.loop(0, pieces)
    def _(p):
        mine = mate[p]
        owner = lax.div(mine, pieces)

        def rank(other, met):
            theirs = mate[other]
            ahead = (lax.div(theirs, pieces) == owner) & (theirs < mine)
            return met + ahead.astype(jnp.int32)

        slots_out[p] = owner * CAP + lax.fori_loop(0, pieces, rank, jnp.int32(0))

    stays.wait()
    keep_coupled.wait()
    for copy in keeps:
        copy.wait()

    @pl.loop(1, n_kin)
    def _(d):
        to_peer(d, lax.rem(kin + d, n_kin), lax.rem(kin + n_kin - d, n_kin)).wait()

    @pl.loop(0, channels)
    def _(c):
        send_inner(c).wait_send()
        for copy in send_rest(c):
            copy.wait()


def finish_kernel(
    orders, partner, listed, slots, energies, coupled, low, right, mlow, mright, incoming, out
):
    c = pl.program_id(0)
    order = out.shape[1]
    tile = order // SIDE
    inner = LISTED * tile
    count = orders[c]
    across = energies[pl.ds(c, 1), :]
    down = jnp.broadcast_to(across, (tile, order)).T

    def scaled(value, i, j):
        rows = slice(i * tile, (i + 1) * tile)
        width = value.shape[1]
        e = down[rows, :]
        if width > tile:
            e = jnp.concatenate([e] * (width // tile), axis=1)
        denominator = e + across[:, j * tile : j * tile + width]
        keep = (lax.broadcasted_iota(jnp.int32, value.shape, 0) + i * tile < count) & (
            lax.broadcasted_iota(jnp.int32, value.shape, 1) + j * tile < count
        )
        return jnp.where(keep, value / denominator, 0.0).astype(BF16)

    def half_sum(own, mirror):
        return (0.5 * (own.astype(F32) + mirror.astype(F32))).astype(BF16).astype(F32)

    for i in range(LISTED):
        rows = slice(i * tile, (i + 1) * tile)
        for j in range(LISTED):
            cols = slice(j * tile, (j + 1) * tile)
            out[0, rows, cols] = scaled(coupled[0, i, j].astype(F32), i, j)
        out[0, rows, inner:] = scaled(half_sum(right[0, rows, :], mright[0, rows, :]), i, LISTED)
    for j in range(SIDE):
        cols = slice(j * tile, (j + 1) * tile)
        out[0, inner:, cols] = scaled(half_sum(low[0, :, cols], mlow[0, :, cols]), LISTED, j)

    @pl.loop(0, listed.shape[0])
    def _(p):
        at = listed[p]
        spot = lax.rem(at, SIDE * SIDE)
        for i in range(LISTED):
            for j in range(LISTED):

                @pl.when((lax.div(at, SIDE * SIDE) == c) & (spot == i * SIDE + j))
                def _():
                    mate = incoming[slots[p]].astype(F32)
                    value = coupled[0, i, j].astype(F32) - mate
                    rows = slice(i * tile, (i + 1) * tile)
                    out[0, rows, j * tile : (j + 1) * tile] = scaled(value, i, j)


def on_device(amplitudes, coulomb, energies, orders, partner, listed, mate_piece):
    channels, order, _ = amplitudes.shape
    tile = order // SIDE
    inner = LISTED * tile
    pieces = listed.shape[0]
    n_chan, n_kin = lax.axis_size("chan"), lax.axis_size("kin")
    block = (channels, LISTED, LISTED, tile, tile)
    low, right = (channels, tile, order), (channels, inner, tile)
    shape = jax.ShapeDtypeStruct
    hbm = pl.BlockSpec(memory_space=pl.ANY)
    smem = pl.BlockSpec(memory_space=pltpu.SMEM)
    dma = pltpu.SemaphoreType.DMA
    coupled, own_low, own_right, mlow, mright, incoming, slots = pl.pallas_call(
        functools.partial(exchange_kernel, n_chan, n_kin),
        out_shape=(
            shape(block, BF16),
            shape(low, BF16),
            shape(right, BF16),
            shape(low, BF16),
            shape(right, BF16),
            shape((n_kin, CAP, tile, tile), BF16),
            shape((pieces,), jnp.int32),
        ),
        in_specs=[smem] * 4 + [hbm] * 2,
        out_specs=[hbm] * 6 + [smem],
        scratch_shapes=[
            pltpu.VMEM((channels, order, order), BF16),
            pltpu.VMEM((channels, order, order), BF16),
            pltpu.VMEM(block, BF16),
            pltpu.VMEM(low, BF16),
            pltpu.VMEM(right, BF16),
            pltpu.VMEM(block, BF16),
            pltpu.VMEM(low, BF16),
            pltpu.VMEM(right, BF16),
            pltpu.VMEM(block, BF16),
            pltpu.VMEM(block, BF16),
            pltpu.VMEM((n_kin, CAP, tile, tile), BF16),
            dma((2, channels)),
            dma((3,)),
            dma((3, channels)),
            dma((3, channels)),
            dma((n_kin,)),
            dma((n_kin,)),
            dma,
        ],
        compiler_params=pltpu.CompilerParams(
            collective_id=0, has_side_effects=True, vmem_limit_bytes=44 << 20
        ),
        name="exchange",
    )(orders, partner, listed, mate_piece, amplitudes, coulomb)
    return pl.pallas_call(
        finish_kernel,
        out_shape=shape(amplitudes.shape, BF16),
        grid_spec=pltpu.PrefetchScalarGridSpec(
            num_scalar_prefetch=4,
            grid=(channels,),
            in_specs=[
                pl.BlockSpec(energies.shape, lambda c, *_: (0, 0)),
                pl.BlockSpec((1, *block[1:]), lambda c, *_: (c, 0, 0, 0, 0)),
                pl.BlockSpec((1, *low[1:]), lambda c, *_: (c, 0, 0)),
                pl.BlockSpec((1, *right[1:]), lambda c, *_: (c, 0, 0)),
                pl.BlockSpec((1, *low[1:]), lambda c, o, p, *_: (lax.rem(p[c], channels), 0, 0)),
                pl.BlockSpec((1, *right[1:]), lambda c, o, p, *_: (lax.rem(p[c], channels), 0, 0)),
                pl.BlockSpec((n_kin * CAP, tile, tile), lambda c, *_: (0, 0, 0)),
            ],
            out_specs=pl.BlockSpec((1, order, order), lambda c, *_: (c, 0, 0)),
        ),
        compiler_params=pltpu.CompilerParams(vmem_limit_bytes=32 << 20),
        name="finish",
    )(
        orders, partner, listed, slots, energies, coupled, own_low, own_right, mlow, mright,
        incoming.reshape(n_kin * CAP, tile, tile),
    )


def solution(mesh):
    whole, rows, flat = P(("chan", "kin"), None, None), P(("chan", "kin"), None), P(("chan", "kin"))
    return jax.shard_map(
        on_device,
        mesh=mesh,
        in_specs=(whole, whole, rows, flat, flat, flat, flat),
        out_specs=whole,
        check_vma=False,
    )
```
